32 devices in a mesh: outer: 8 (over z, x), inner: 4 (over y, core).
Axes of the slice: x: 2, y: 2, z: 4, core: 2. Of those that a mesh axis runs over, the one named last changes fastest.
Arguments:
- queries: bfloat16 [4096, 128], P('inner'), may hold values from -150 to 150
- key_rows: bfloat16 [8192, 128], P(('outer', 'inner')), may hold values from -4.5 to 4.5
- value_rows: bfloat16 [8192, 128], P(('outer', 'inner')), may hold values from -6 to 6
Outputs:
- attended: bfloat16 [4096, 128], P('inner')
The draws below stay inside these ranges and needn't reach their ends.
All inputs are finite; a program needn't handle non-finite values.
Results may differ from the reference program's by a relative error of at most 0.015.
Values may be sent and summed in bfloat16 or wider, within the bound.
A program may use at most 64 MiB of HBM per device.

```python
import math
import jax
import jax.numpy as jnp
from jax import lax

HD = 128
QUERIES = 4096
KEYS = 8192


def draw_queries(key, part):
    limit = float(min(300, 16384 // HD + 22))
    spread = jnp.exp(jax.random.uniform(jax.random.fold_in(key, 9), (QUERIES, 1), jnp.float32, math.log(3.5), math.log(40.0)))
    entries = jnp.clip(spread * jax.random.normal(jax.random.fold_in(key, 5), (QUERIES, HD), jnp.float32), -limit, limit)
    return entries.astype(jnp.bfloat16)


def draw_key_rows(key, part):
    entries = jnp.clip(jax.random.normal(jax.random.fold_in(key, 7), (KEYS, HD), jnp.float32), -4.5, 4.5)
    return entries.astype(jnp.bfloat16)


def steps_of(key, shape, split, least, high):
    gain = 1.0
    for axis_at, shards_of in split:
        draws = jax.random.uniform(jax.random.fold_in(jax.random.fold_in(key, 6), axis_at), (shards_of,), jnp.float32, least / len(split), high / len(split))
        gain = gain * jnp.repeat(jnp.exp(draws), shape[axis_at] // shards_of).reshape((-1,) + (1,) * (len(shape) - 1 - axis_at))
    return gain


def normal_values(own_key, extent, width, most, pieces=(), dtype=jnp.bfloat16):
    gain = steps_of(own_key, extent, pieces, -0.22, 0.18) if pieces else 1.0
    result = jax.random.normal(own_key, extent, jnp.float32) * width * gain
    return jnp.minimum(jnp.maximum(result, -most), most).astype(dtype)


def setup_inputs(seed: int = 0) -> dict:
    arg_keys = jax.random.split(jax.random.key(seed), 4)
    queries = draw_queries(jax.random.fold_in(arg_keys[3], 71), 0)
    key_rows = draw_key_rows(jax.random.fold_in(arg_keys[3], 71), 0)
    value_rows = normal_values(arg_keys[2], (KEYS, HD), 1.0, 6.0, ((0, 32),))
    return {"queries": queries, "key_rows": key_rows, "value_rows": value_rows}


def reference(queries, key_rows, value_rows):
    score_scale = 1.0 / math.sqrt(HD)
    block_rows = math.gcd(QUERIES, 256)

    def attend_block(query_block):
        scores = jnp.dot(query_block, key_rows.T, preferred_element_type=jnp.float32) * score_scale
        row_peak = lax.optimization_barrier(jnp.max(scores, axis=1))
        probs = jnp.exp(scores - row_peak[:, None])
        row_total = lax.optimization_barrier(jnp.sum(probs, axis=1))
        numerator = jnp.dot(probs.astype(jnp.bfloat16), value_rows, preferred_element_type=jnp.float32)
        return (numerator / row_total[:, None]).astype(jnp.bfloat16)
    blocks = queries.reshape(QUERIES // block_rows, block_rows, HD)
    return lax.map(attend_block, blocks).reshape(QUERIES, HD)
```

```python
import functools
import math

import jax
import jax.numpy as jnp
from jax import lax
from jax.experimental import pallas as pl
from jax.experimental.pallas import tpu as pltpu
from jax.sharding import PartitionSpec as P

MESH = pl.DeviceIdType.MESH
K, V = 0, 1


def kernel(outer_size, inner_size, q_hbm, k_hbm, v_hbm, out_ref, q_vm, kv, send_acc, recv_acc,
           send_stat, recv_stat, local_sem, kv_send, kv_recv, z_send, z_recv, g_send, g_recv):
    nz, ny = outer_size // 2, inner_size // 2
    queries, head = out_ref.shape
    half = queries // 2
    rows = half // nz
    outer, inner = lax.axis_index("outer"), lax.axis_index("inner")
    z, x = outer // 2, outer % 2
    y, core = inner // 2, inner % 2

    x_peer = (z * 2 + (1 - x), inner)
    sibling = (outer, y * 2 + (1 - core))

    def y_peer(j):
        return (outer, lax.rem(y + j, ny) * 2 + core)

    def z_peer(j):
        return (lax.rem(z + j, nz) * 2 + x, inner)

    local = [
        pltpu.make_async_copy(k_hbm, kv.at[0, 0, K, 0], local_sem.at[0]),
        pltpu.make_async_copy(q_hbm.at[pl.ds(pl.multiple_of(x * half, half), half)], q_vm, local_sem.at[1]),
        pltpu.make_async_copy(v_hbm, kv.at[0, 0, V, 0], local_sem.at[2]),
    ]
    for copy in local:
        copy.start()

    barrier = pltpu.get_barrier_semaphore()
    peers = [x_peer, sibling] + [y_peer(j) for j in range(1, ny)] + [z_peer(j) for j in range(1, nz)]
    for peer in peers:
        pl.semaphore_signal(barrier, inc=1, device_id=peer, device_id_type=MESH)
    pl.semaphore_wait(barrier, len(peers))

    flying = {}

    def send(src, slot, peer):
        copy = pltpu.make_async_remote_copy(
            src_ref=src,
            dst_ref=kv.at[slot],
            send_sem=kv_send.at[slot],
            recv_sem=kv_recv.at[slot],
            device_id=peer,
            device_id_type=MESH,
        )
        copy.start()
        flying[slot] = copy

    def arrive(*slot):
        flying[slot].wait_recv()

    send(k_hbm, (1, 0, K, 0), x_peer)
    for j in range(1, ny):
        send(v_hbm, (0, ny - j, V, 0), y_peer(j))
    send(k_hbm, (0, 0, K, 1), sibling)
    send(v_hbm, (0, 0, V, 1), sibling)
    send(v_hbm, (1, 0, V, 0), x_peer)
    for j in range(1, ny):
        send(k_hbm, (0, ny - j, K, 0), y_peer(j))

    to_exponent = math.log2(math.e) / math.sqrt(head)

    def advance(state, keys, values):
        scores = lax.dot_general(
            keys, q_vm[...], (((1,), (1,)), ((), ())), preferred_element_type=jnp.float32
        ) * to_exponent
        peak = jnp.max(scores, axis=0, keepdims=True)
        if state is not None:
            peak = jnp.maximum(peak, state[1])
        probs = jnp.exp2(scores - peak)
        total = jnp.sum(probs, axis=0, keepdims=True)
        weighted = lax.dot_general(
            values, probs.astype(jnp.bfloat16), (((0,), (0,)), ((), ())), preferred_element_type=jnp.float32
        )
        if state is not None:
            factor = jnp.exp2(state[1] - peak)
            weighted = weighted + state[0] * factor
            total = total + state[2] * factor
        return weighted, peak, total

    def one(state, xr, yr, c):
        return advance(state, kv[xr, yr, K, c], kv[xr, yr, V, c])

    def chip(state, xr, yr):
        return advance(
            state, kv[xr, yr, K].reshape(-1, head), kv[xr, yr, V].reshape(-1, head)
        )

    for copy in local:
        copy.wait()
    state = one(None, 0, 0, 0)
    arrive(0, 0, K, 1)
    arrive(0, 0, V, 1)
    state = one(state, 0, 0, 1)

    arrive(1, 0, K, 0)
    for j in range(1, ny):
        send(kv.at[1, 0, K, 0], (1, ny - j, K, 0), y_peer(j))
    send(kv.at[1, 0, K, 0], (1, 0, K, 1), sibling)
    for yr in range(ny - 1, 0, -1):
        arrive(0, yr, V, 0)
        send(kv.at[0, yr, V, 0], (1, yr, V, 0), x_peer)
        send(kv.at[0, yr, V, 0], (0, yr, V, 1), sibling)
    arrive(1, 0, V, 0)
    send(kv.at[1, 0, V, 0], (1, 0, V, 1), sibling)
    for yr in range(ny - 1, 0, -1):
        arrive(0, yr, K, 0)
        send(kv.at[0, yr, K, 0], (0, yr, K, 1), sibling)
    arrive(1, 0, K, 1)
    arrive(1, 0, V, 1)
    state = chip(state, 1, 0)
    for yr in range(ny - 1, 0, -1):
        arrive(0, yr, K, 1)
        arrive(0, yr, V, 1)
        state = chip(state, 0, yr)
    for yr in range(ny - 1, 0, -1):
        for which in (K, V):
            arrive(1, yr, which, 0)
            send(kv.at[1, yr, which, 0], (1, yr, which, 1), sibling)
        state = one(state, 1, yr, 0)
    for yr in range(ny - 1, 0, -1):
        for which in (K, V):
            arrive(1, yr, which, 1)
        state = one(state, 1, yr, 1)

    weighted, peak, total = state
    is_peak = lax.broadcasted_iota(jnp.int32, (8, half), 0) < 4
    stat = jnp.where(is_peak, peak, total)
    for zt in range(nz):
        send_acc[zt] = weighted[:, zt * rows:(zt + 1) * rows].astype(jnp.bfloat16)
        send_stat[zt] = stat[:, zt * rows:(zt + 1) * rows]
    parts = []
    for j in range(1, nz):
        target = lax.rem(z + j, nz)
        for at, (src, dst) in enumerate(((send_stat, recv_stat), (send_acc, recv_acc))):
            copy = pltpu.make_async_remote_copy(
                src_ref=src.at[target],
                dst_ref=dst.at[nz - j],
                send_sem=z_send.at[j, at],
                recv_sem=z_recv.at[nz - j, at],
                device_id=z_peer(j),
                device_id_type=MESH,
            )
            copy.start()
            parts.append(copy)
    for copy in parts:
        copy.wait_recv()
    stats = [send_stat[z]] + [recv_stat[s] for s in range(1, nz)]
    sums = [send_acc[z]] + [recv_acc[s] for s in range(1, nz)]
    joint_peak = functools.reduce(jnp.maximum, [s[0:1] for s in stats])
    joint_total = jnp.zeros_like(joint_peak)
    joint_sum = jnp.zeros((head, rows), jnp.float32)
    for s, a in zip(stats, sums):
        factor = jnp.exp2(s[0:1] - joint_peak)
        joint_total = joint_total + s[4:5] * factor
        joint_sum = joint_sum + a.astype(jnp.float32) * factor

    def block(xr, source):
        return out_ref.at[pl.ds(pl.multiple_of((xr * nz + source) * rows, rows), rows)]

    mine = block(x, z)
    mine[...] = (joint_sum / joint_total).T.astype(jnp.bfloat16)

    def share(view, xr, zr, peer):
        copy = pltpu.make_async_remote_copy(
            src_ref=view,
            dst_ref=view,
            send_sem=g_send.at[xr, zr],
            recv_sem=g_recv.at[xr, zr],
            device_id=peer,
            device_id_type=MESH,
        )
        copy.start()
        return copy

    across = [share(mine, 1, 0, x_peer)]
    along = [share(mine, 0, nz - j, z_peer(j)) for j in range(1, nz)]
    for j in range(1, nz):
        along[j - 1].wait_recv()
        across.append(share(block(x, lax.rem(z + nz - j, nz)), 1, nz - j, x_peer))
    for copy in across:
        copy.wait_recv()
    for copy in list(flying.values()) + parts + along + across:
        copy.wait_send()


def on_device(outer_size, inner_size, queries, key_rows, value_rows):
    count, head = queries.shape
    keys = key_rows.shape[0]
    nz, ny = outer_size // 2, inner_size // 2
    rows = count // 2 // nz
    dma = pltpu.SemaphoreType.DMA
    return pl.pallas_call(
        functools.partial(kernel, outer_size, inner_size),
        out_shape=jax.ShapeDtypeStruct((count, head), jnp.bfloat16),
        in_specs=[pl.BlockSpec(memory_space=pl.ANY)] * 3,
        out_specs=pl.BlockSpec(memory_space=pltpu.VMEM),
        scratch_shapes=[
            pltpu.VMEM((count // 2, head), jnp.bfloat16),
            pltpu.VMEM((2, ny, 2, 2, keys, head), jnp.bfloat16),
            pltpu.VMEM((nz, head, rows), jnp.bfloat16),
            pltpu.VMEM((nz, head, rows), jnp.bfloat16),
            pltpu.VMEM((nz, 8, rows), jnp.float32),
            pltpu.VMEM((nz, 8, rows), jnp.float32),
            dma((3,)),
            dma((2, ny, 2, 2)),
            dma((2, ny, 2, 2)),
            dma((nz, 2)),
            dma((nz, 2)),
            dma((2, nz)),
            dma((2, nz)),
        ],
        compiler_params=pltpu.CompilerParams(
            collective_id=0, has_side_effects=True, vmem_limit_bytes=48 * 1024 * 1024
        ),
        cost_estimate=pl.CostEstimate(
            flops=2 * count * keys * inner_size * head * 2,
            bytes_accessed=2 * (2 * count + 2 * keys) * head,
            transcendentals=count * keys * inner_size,
        ),
    )(queries, key_rows, value_rows)


def solution(mesh):
    return jax.shard_map(
        functools.partial(on_device, mesh.shape["outer"], mesh.shape["inner"]),
        mesh=mesh,
        in_specs=(P("inner", None), P(("outer", "inner"), None), P(("outer", "inner"), None)),
        out_specs=P("inner", None),
        check_vma=False,
    )
```

```python
import functools
import math

import jax
import jax.numpy as jnp
from jax import lax
from jax.experimental import pallas as pl
from jax.experimental.pallas import tpu as pltpu
from jax.sharding import PartitionSpec as P

MESH = pl.DeviceIdType.MESH
K, V = 0, 1


def kernel(outer_size, inner_size, q_hbm, k_hbm, v_hbm, out_ref, q_vm, kv, sum_ref, peak_ref, total_ref,
           send_acc, recv_acc, send_stat, recv_stat, local_sem, kv_send, kv_recv, z_send, z_recv, g_send, g_recv):
    nz, ny = outer_size // 2, inner_size // 2
    queries, head = out_ref.shape
    half = queries // 2
    rows = half // nz
    outer, inner = lax.axis_index("outer"), lax.axis_index("inner")
    z, x = outer // 2, outer % 2
    y, core = inner // 2, inner % 2

    x_peer = (z * 2 + (1 - x), inner)
    sibling = (outer, y * 2 + (1 - core))
    y_peers = [None] + [(outer, lax.rem(y + j, ny) * 2 + core) for j in range(1, ny)]
    z_peers = [None] + [(lax.rem(z + j, nz) * 2 + x, inner) for j in range(1, nz)]

    def z_peer(j):
        return z_peers[j]

    def slot_of(xr, yr, c):
        chip = (xr if yr == 0 else 1 + yr) if xr == 0 or yr == 0 else ny + yr
        return chip * 2 + c

    local = [
        pltpu.make_async_copy(k_hbm, kv.at[0, K], local_sem.at[0]),
        pltpu.make_async_copy(v_hbm, kv.at[0, V], local_sem.at[1]),
        pltpu.make_async_copy(q_hbm.at[pl.ds(pl.multiple_of(x * half, half), half)], q_vm, local_sem.at[2]),
    ]
    for copy in local:
        copy.start()

    barrier = pltpu.get_barrier_semaphore()
    peers = [x_peer, sibling] + y_peers[1:] + z_peers[1:]
    for peer in peers:
        pl.semaphore_signal(barrier, inc=1, device_id=peer, device_id_type=MESH)
    peak_ref[...] = jnp.full_like(peak_ref, -1e30)
    total_ref[...] = jnp.zeros_like(total_ref)
    sum_ref[...] = jnp.zeros_like(sum_ref)
    local[0].wait()
    local[1].wait()
    pl.semaphore_wait(barrier, len(peers))

    def copy_of(source, slot, which, peer):
        return pltpu.make_async_remote_copy(
            src_ref=kv.at[source, which],
            dst_ref=kv.at[slot, which],
            send_sem=kv_send.at[slot, which],
            recv_sem=kv_recv.at[slot, which],
            device_id=peer,
            device_id_type=MESH,
        )

    def arrive(slot, which):
        copy_of(0, slot, which, sibling).wait_recv()

    def to_sibling(slot, which):
        copy_of(slot, slot + 1, which, sibling).start()

    copy_of(0, slot_of(1, 0, 0), K, x_peer).start()
    for j in range(1, ny):
        copy_of(0, slot_of(0, ny - j, 0), V, y_peers[j]).start()
    to_sibling(0, K)
    to_sibling(0, V)
    copy_of(0, slot_of(1, 0, 0), V, x_peer).start()
    for j in range(1, ny):
        copy_of(0, slot_of(0, ny - j, 0), K, y_peers[j]).start()
    local[2].wait()

    def first_arrivals():
        beside = slot_of(1, 0, 0)
        arrive(beside, K)
        for j in range(1, ny):
            copy_of(beside, slot_of(1, ny - j, 0), K, y_peers[j]).start()
        to_sibling(beside, K)
        for yr in range(ny - 1, 0, -1):
            along = slot_of(0, yr, 0)
            arrive(along, V)
            copy_of(along, slot_of(1, yr, 0), V, x_peer).start()
            to_sibling(along, V)
        arrive(beside, V)
        to_sibling(beside, V)
        for yr in range(ny - 1, 0, -1):
            along = slot_of(0, yr, 0)
            arrive(along, K)
            to_sibling(along, K)

    to_exponent = math.log2(math.e) / math.sqrt(head)

    def step(t, carry):
        pl.when(t == 2)(first_arrivals)
        for yr in range(1, ny):
            @pl.when(t == slot_of(1, yr, 0))
            def _():
                for which in (K, V):
                    arrive(slot_of(1, yr, 0), which)
                    to_sibling(slot_of(1, yr, 0), which)

        @pl.when(t % 2 == 1)
        def _():
            arrive(t, K)
            arrive(t, V)

        scores = lax.dot_general(
            kv[t, K], q_vm[...], (((1,), (1,)), ((), ())), preferred_element_type=jnp.float32
        ) * to_exponent
        peak = jnp.maximum(peak_ref[...], jnp.max(scores, axis=0, keepdims=True))
        factor = jnp.exp2(peak_ref[...] - peak)
        probs = jnp.exp2(scores - peak)
        peak_ref[...] = peak
        total_ref[...] = total_ref[...] * factor + jnp.sum(probs, axis=0, keepdims=True)
        sum_ref[...] = sum_ref[...] * factor + lax.dot_general(
            kv[t, V], probs.astype(jnp.bfloat16), (((0,), (0,)), ((), ())), preferred_element_type=jnp.float32
        )
        return carry

    lax.fori_loop(0, 4 * ny, step, 0)

    weighted, peak, total = sum_ref[...], peak_ref[...], total_ref[...]
    is_peak = lax.broadcasted_iota(jnp.int32, (8, half), 0) < 4
    stat = jnp.where(is_peak, peak, total)
    for zt in range(nz):
        send_acc[zt] = weighted[:, zt * rows:(zt + 1) * rows].astype(jnp.bfloat16)
        send_stat[zt] = stat[:, zt * rows:(zt + 1) * rows]
    parts = []
    for j in range(1, nz):
        target = lax.rem(z + j, nz)
        for at, (src, dst) in enumerate(((send_stat, recv_stat), (send_acc, recv_acc))):
            copy = pltpu.make_async_remote_copy(
                src_ref=src.at[target],
                dst_ref=dst.at[nz - j],
                send_sem=z_send.at[j, at],
                recv_sem=z_recv.at[nz - j, at],
                device_id=z_peer(j),
                device_id_type=MESH,
            )
            copy.start()
            parts.append(copy)
    for copy in parts:
        copy.wait_recv()
    stats = [send_stat[z]] + [recv_stat[s] for s in range(1, nz)]
    sums = [send_acc[z]] + [recv_acc[s] for s in range(1, nz)]
    joint_peak = functools.reduce(jnp.maximum, [s[0:1] for s in stats])
    joint_total = jnp.zeros_like(joint_peak)
    joint_sum = jnp.zeros((head, rows), jnp.float32)
    for s, a in zip(stats, sums):
        factor = jnp.exp2(s[0:1] - joint_peak)
        joint_total = joint_total + s[4:5] * factor
        joint_sum = joint_sum + a.astype(jnp.float32) * factor

    def block(xr, source):
        return out_ref.at[pl.ds(pl.multiple_of((xr * nz + source) * rows, rows), rows)]

    mine = block(x, z)
    mine[...] = (joint_sum / joint_total).T.astype(jnp.bfloat16)

    def share(view, xr, zr, peer):
        copy = pltpu.make_async_remote_copy(
            src_ref=view,
            dst_ref=view,
            send_sem=g_send.at[xr, zr],
            recv_sem=g_recv.at[xr, zr],
            device_id=peer,
            device_id_type=MESH,
        )
        copy.start()
        return copy

    across = [share(mine, 1, 0, x_peer)]
    along = [share(mine, 0, nz - j, z_peer(j)) for j in range(1, nz)]
    for j in range(1, nz):
        along[j - 1].wait_recv()
        across.append(share(block(x, lax.rem(z + nz - j, nz)), 1, nz - j, x_peer))
    for copy in across:
        copy.wait_recv()
    for copy in parts + along + across:
        copy.wait_send()
    for slot in range(1, 4 * ny):
        for which in (K, V):
            copy_of(0, slot, which, sibling).wait_send()


def on_device(outer_size, inner_size, queries, key_rows, value_rows):
    count, head = queries.shape
    keys = key_rows.shape[0]
    nz, ny = outer_size // 2, inner_size // 2
    rows = count // 2 // nz
    dma = pltpu.SemaphoreType.DMA
    return pl.pallas_call(
        functools.partial(kernel, outer_size, inner_size),
        out_shape=jax.ShapeDtypeStruct((count, head), jnp.bfloat16),
        in_specs=[pl.BlockSpec(memory_space=pltpu.HBM)] * 3,
        out_specs=pl.BlockSpec(memory_space=pltpu.VMEM),
        scratch_shapes=[
            pltpu.VMEM((count // 2, head), jnp.bfloat16),
            pltpu.VMEM((4 * ny, 2, keys, head), jnp.bfloat16),
            pltpu.VMEM((head, count // 2), jnp.float32),
            pltpu.VMEM((1, count // 2), jnp.float32),
            pltpu.VMEM((1, count // 2), jnp.float32),
            pltpu.VMEM((nz, head, rows), jnp.bfloat16),
            pltpu.VMEM((nz, head, rows), jnp.bfloat16),
            pltpu.VMEM((nz, 8, rows), jnp.float32),
            pltpu.VMEM((nz, 8, rows), jnp.float32),
            dma((3,)),
            dma((4 * ny, 2)),
            dma((4 * ny, 2)),
            dma((nz, 2)),
            dma((nz, 2)),
            dma((2, nz)),
            dma((2, nz)),
        ],
        compiler_params=pltpu.CompilerParams(
            collective_id=0, has_side_effects=True, vmem_limit_bytes=48 * 1024 * 1024
        ),
        cost_estimate=pl.CostEstimate(
            flops=2 * count * keys * inner_size * head * 2,
            bytes_accessed=2 * (2 * count + 2 * keys) * head,
            transcendentals=count * keys * inner_size,
        ),
    )(*(pltpu.with_memory_space_constraint(a, pltpu.HBM) for a in (queries, key_rows, value_rows)))


def solution(mesh):
    return jax.shard_map(
        functools.partial(on_device, mesh.shape["outer"], mesh.shape["inner"]),
        mesh=mesh,
        in_specs=(P("inner", None), P(("outer", "inner"), None), P(("outer", "inner"), None)),
        out_specs=P("inner", None),
        check_vma=False,
    )
```

```python
import functools
import math

import jax
import jax.numpy as jnp
from jax import lax
from jax.experimental import pallas as pl
from jax.experimental.pallas import tpu as pltpu
from jax.sharding import PartitionSpec as P

MESH = pl.DeviceIdType.MESH
K, V = 0, 1


def kernel(outer_size, inner_size, q_hbm, k_hbm, v_hbm, out_ref, q_vm, kv, sum_ref, peak_ref, total_ref,
           send_acc, recv_acc, send_stat, recv_stat, local_sem, kv_send, kv_recv, z_send, z_recv, g_send, g_recv):
    nz, ny = outer_size // 2, inner_size // 2
    queries, head = out_ref.shape
    half = queries // 2
    rows = half // nz
    outer, inner = lax.axis_index("outer"), lax.axis_index("inner")
    z, x = outer // 2, outer % 2
    y, core = inner // 2, inner % 2

    x_peer = (z * 2 + (1 - x), inner)
    sibling = (outer, y * 2 + (1 - core))
    y_peers = [None] + [(outer, lax.rem(y + j, ny) * 2 + core) for j in range(1, ny)]
    z_peers = [None] + [(lax.rem(z + j, nz) * 2 + x, inner) for j in range(1, nz)]

    def z_peer(j):
        return z_peers[j]

    def slot_of(xr, yr, c):
        chip = (xr if yr == 0 else 1 + yr) if xr == 0 or yr == 0 else ny + yr
        return chip * 2 + c

    local = [
        pltpu.make_async_copy(k_hbm, kv.at[0, K], local_sem.at[0]),
        pltpu.make_async_copy(v_hbm, kv.at[0, V], local_sem.at[1]),
        pltpu.make_async_copy(q_hbm.at[pl.ds(pl.multiple_of(x * half, half), half)], q_vm, local_sem.at[2]),
    ]
    for copy in local:
        copy.start()

    barrier = pltpu.get_barrier_semaphore()
    peers = [x_peer, sibling] + y_peers[1:] + z_peers[1:]
    for peer in peers:
        pl.semaphore_signal(barrier, inc=1, device_id=peer, device_id_type=MESH)
    peak_ref[...] = jnp.full_like(peak_ref, -1e30)
    total_ref[...] = jnp.zeros_like(total_ref)
    sum_ref[...] = jnp.zeros_like(sum_ref)
    local[0].wait()
    local[1].wait()
    pl.semaphore_wait(barrier, len(peers))

    def copy_of(source, slot, which, peer):
        return pltpu.make_async_remote_copy(
            src_ref=kv.at[source, which],
            dst_ref=kv.at[slot, which],
            send_sem=kv_send.at[slot, which],
            recv_sem=kv_recv.at[slot, which],
            device_id=peer,
            device_id_type=MESH,
        )

    def arrive(slot, which):
        copy_of(0, slot, which, sibling).wait_recv()

    def to_sibling(slot, which):
        copy_of(slot, slot + 1, which, sibling).start()

    copy_of(0, slot_of(1, 0, 0), K, x_peer).start()
    for j in range(1, ny):
        copy_of(0, slot_of(0, ny - j, 0), V, y_peers[j]).start()
    to_sibling(0, K)
    to_sibling(0, V)
    local[2].wait()
    sent_early = [(slot_of(1, 0, 0), K)] + [(slot_of(0, yr, 0), V) for yr in range(1, ny)]

    def second_sends():
        for slot, which in sent_early:
            copy_of(0, slot, which, sibling).wait_send()
        copy_of(0, slot_of(1, 0, 0), V, x_peer).start()
        for j in range(1, ny):
            copy_of(0, slot_of(0, ny - j, 0), K, y_peers[j]).start()

    def first_arrivals():
        beside = slot_of(1, 0, 0)
        arrive(beside, K)
        for j in range(1, ny):
            copy_of(beside, slot_of(1, ny - j, 0), K, y_peers[j]).start()
        to_sibling(beside, K)
        for yr in range(ny - 1, 0, -1):
            along = slot_of(0, yr, 0)
            arrive(along, V)
            copy_of(along, slot_of(1, yr, 0), V, x_peer).start()
            to_sibling(along, V)
        arrive(beside, V)
        to_sibling(beside, V)
        for yr in range(ny - 1, 0, -1):
            along = slot_of(0, yr, 0)
            arrive(along, K)
            to_sibling(along, K)

    to_exponent = math.log2(math.e) / math.sqrt(head)

    def step(t, carry):
        pl.when(t == 1)(second_sends)
        pl.when(t == 2)(first_arrivals)
        for yr in range(1, ny):
            @pl.when(t == slot_of(1, yr, 0))
            def _():
                for which in (K, V):
                    arrive(slot_of(1, yr, 0), which)
                    to_sibling(slot_of(1, yr, 0), which)

        @pl.when(t % 2 == 1)
        def _():
            arrive(t, K)
            arrive(t, V)

        scores = lax.dot_general(
            kv[t, K], q_vm[...], (((1,), (1,)), ((), ())), preferred_element_type=jnp.float32
        ) * to_exponent
        peak = jnp.maximum(peak_ref[...], jnp.max(scores, axis=0, keepdims=True))
        factor = jnp.exp2(peak_ref[...] - peak)
        probs = jnp.exp2(scores - peak)
        peak_ref[...] = peak
        total_ref[...] = total_ref[...] * factor + jnp.sum(probs, axis=0, keepdims=True)
        sum_ref[...] = sum_ref[...] * factor + lax.dot_general(
            kv[t, V], probs.astype(jnp.bfloat16), (((0,), (0,)), ((), ())), preferred_element_type=jnp.float32
        )
        return carry

    lax.fori_loop(0, 4 * ny, step, 0)

    weighted, peak, total = sum_ref[...], peak_ref[...], total_ref[...]
    is_peak = lax.broadcasted_iota(jnp.int32, (8, half), 0) < 4
    stat = jnp.where(is_peak, peak, total)
    for zt in range(nz):
        send_acc[zt] = weighted[:, zt * rows:(zt + 1) * rows].astype(jnp.bfloat16)
        send_stat[zt] = stat[:, zt * rows:(zt + 1) * rows]
    parts = []
    for j in range(1, nz):
        target = lax.rem(z + j, nz)
        for at, (src, dst) in enumerate(((send_stat, recv_stat), (send_acc, recv_acc))):
            copy = pltpu.make_async_remote_copy(
                src_ref=src.at[target],
                dst_ref=dst.at[nz - j],
                send_sem=z_send.at[j, at],
                recv_sem=z_recv.at[nz - j, at],
                device_id=z_peer(j),
                device_id_type=MESH,
            )
            copy.start()
            parts.append(copy)
    for copy in parts:
        copy.wait_recv()
    stats = [send_stat[z]] + [recv_stat[s] for s in range(1, nz)]
    sums = [send_acc[z]] + [recv_acc[s] for s in range(1, nz)]
    joint_peak = functools.reduce(jnp.maximum, [s[0:1] for s in stats])
    joint_total = jnp.zeros_like(joint_peak)
    joint_sum = jnp.zeros((head, rows), jnp.float32)
    for s, a in zip(stats, sums):
        factor = jnp.exp2(s[0:1] - joint_peak)
        joint_total = joint_total + s[4:5] * factor
        joint_sum = joint_sum + a.astype(jnp.float32) * factor

    def block(xs, zs):
        return out_ref.at[pl.ds(pl.multiple_of((xs * nz + zs) * rows, rows), rows)]

    def share(xr, zs, peer, way):
        xs = x if way == "z" and xr == 0 or way == "x" and xr == 1 else 1 - x
        return pltpu.make_async_remote_copy(
            src_ref=block(xs, zs),
            dst_ref=block(xs, zs),
            send_sem=g_send.at[0 if way == "z" else 1, len(shared)],
            recv_sem=g_recv.at[xr, zs],
            device_id=peer,
            device_id_type=MESH,
        )

    shared = []

    def begin(*args):
        copy = share(*args)
        copy.start()
        shared.append(copy)

    def landed(xr, zs):
        share(xr, zs, x_peer, "z").wait_recv()

    block(x, z)[...] = (joint_sum / joint_total).T.astype(jnp.bfloat16)
    near = z + 1 - 2 * (z % 2)
    far = [(lax.rem(z // 2 + p, nz // 2) * 2 + b) for p in range(1, nz // 2) for b in range(2)]
    begin(1, z, x_peer, "x")
    for zt in far + [near]:
        begin(0, z, (zt * 2 + x, inner), "z")
    landed(1, z)
    begin(1, z, (near * 2 + x, inner), "z")
    for zs in far:
        landed(0, zs)
        begin(1, zs, x_peer, "x")
    landed(0, near)
    for zs in [near] + far:
        landed(1, zs)
    for copy in parts + shared:
        copy.wait_send()
    for slot in range(1, 4 * ny):
        for which in (K, V):
            if (slot, which) in sent_early:
                continue
            copy_of(0, slot, which, sibling).wait_send()


def on_device(outer_size, inner_size, queries, key_rows, value_rows):
    count, head = queries.shape
    keys = key_rows.shape[0]
    nz, ny = outer_size // 2, inner_size // 2
    rows = count // 2 // nz
    dma = pltpu.SemaphoreType.DMA
    return pl.pallas_call(
        functools.partial(kernel, outer_size, inner_size),
        out_shape=jax.ShapeDtypeStruct((count, head), jnp.bfloat16),
        in_specs=[pl.BlockSpec(memory_space=pltpu.HBM)] * 3,
        out_specs=pl.BlockSpec(memory_space=pltpu.VMEM),
        scratch_shapes=[
            pltpu.VMEM((count // 2, head), jnp.bfloat16),
            pltpu.VMEM((4 * ny, 2, keys, head), jnp.bfloat16),
            pltpu.VMEM((head, count // 2), jnp.float32),
            pltpu.VMEM((1, count // 2), jnp.float32),
            pltpu.VMEM((1, count // 2), jnp.float32),
            pltpu.VMEM((nz, head, rows), jnp.bfloat16),
            pltpu.VMEM((nz, head, rows), jnp.bfloat16),
            pltpu.VMEM((nz, 8, rows), jnp.float32),
            pltpu.VMEM((nz, 8, rows), jnp.float32),
            dma((3,)),
            dma((4 * ny, 2)),
            dma((4 * ny, 2)),
            dma((nz, 2)),
            dma((nz, 2)),
            dma((2, 2 * nz)),
            dma((2, nz)),
        ],
        compiler_params=pltpu.CompilerParams(
            collective_id=0, has_side_effects=True, vmem_limit_bytes=48 * 1024 * 1024
        ),
        cost_estimate=pl.CostEstimate(
            flops=2 * count * keys * inner_size * head * 2,
            bytes_accessed=2 * (2 * count + 2 * keys) * head,
            transcendentals=count * keys * inner_size,
        ),
    )(*(pltpu.with_memory_space_constraint(a, pltpu.HBM) for a in (queries, key_rows, value_rows)))


def solution(mesh):
    return jax.shard_map(
        functools.partial(on_device, mesh.shape["outer"], mesh.shape["inner"]),
        mesh=mesh,
        in_specs=(P("inner", None), P(("outer", "inner"), None), P(("outer", "inner"), None)),
        out_specs=P("inner", None),
        check_vma=False,
    )
```

```python
import functools
import math

import jax
import jax.numpy as jnp
from jax import lax
from jax.experimental import pallas as pl
from jax.experimental.pallas import tpu as pltpu
from jax.sharding import PartitionSpec as P

MESH = pl.DeviceIdType.MESH
K, V = 0, 1


def kernel(outer_size, inner_size, q_hbm, k_hbm, v_hbm, out_ref, q_vm, kv, sum_ref, peak_ref, total_ref,
           send_acc, recv_acc, send_stat, recv_stat, local_sem, kv_send, kv_recv, z_send, z_recv, g_send, g_recv):
    nz, ny = outer_size // 2, inner_size // 2
    queries, head = out_ref.shape
    half = queries // 2
    rows = half // nz
    outer, inner = lax.axis_index("outer"), lax.axis_index("inner")
    z, x = outer // 2, outer % 2
    y, core = inner // 2, inner % 2

    x_peer = (z * 2 + (1 - x), inner)
    sibling = (outer, y * 2 + (1 - core))
    y_peers = [None] + [(outer, lax.rem(y + j, ny) * 2 + core) for j in range(1, ny)]
    z_peers = [None] + [(lax.rem(z + j, nz) * 2 + x, inner) for j in range(1, nz)]

    def z_peer(j):
        return z_peers[j]

    def slot_of(xr, yr, c):
        chip = (xr if yr == 0 else 1 + yr) if xr == 0 or yr == 0 else ny + yr
        return chip * 2 + c

    local = [
        pltpu.make_async_copy(k_hbm, kv.at[0, K], local_sem.at[0]),
        pltpu.make_async_copy(v_hbm, kv.at[0, V], local_sem.at[1]),
        pltpu.make_async_copy(q_hbm.at[pl.ds(pl.multiple_of(x * half, half), half)], q_vm, local_sem.at[2]),
    ]
    for copy in local:
        copy.start()

    barrier = pltpu.get_barrier_semaphore()
    peers = [x_peer, sibling] + y_peers[1:] + z_peers[1:]
    for peer in peers:
        pl.semaphore_signal(barrier, inc=1, device_id=peer, device_id_type=MESH)
    peak_ref[...] = jnp.full_like(peak_ref, -1e30)
    total_ref[...] = jnp.zeros_like(total_ref)
    sum_ref[...] = jnp.zeros_like(sum_ref)
    local[0].wait()
    local[1].wait()
    pl.semaphore_wait(barrier, len(peers))

    def copy_of(source, slot, which, peer):
        return pltpu.make_async_remote_copy(
            src_ref=kv.at[source, which],
            dst_ref=kv.at[slot, which],
            send_sem=kv_send.at[slot, which],
            recv_sem=kv_recv.at[slot, which],
            device_id=peer,
            device_id_type=MESH,
        )

    def arrive(slot, which):
        copy_of(0, slot, which, sibling).wait_recv()

    def to_sibling(slot, which):
        copy_of(slot, slot + 1, which, sibling).start()

    copy_of(0, slot_of(1, 0, 0), K, x_peer).start()
    for j in range(1, ny):
        copy_of(0, slot_of(0, ny - j, 0), V, y_peers[j]).start()
    to_sibling(0, K)
    to_sibling(0, V)
    local[2].wait()
    sent_early = [(slot_of(1, 0, 0), K)] + [(slot_of(0, yr, 0), V) for yr in range(1, ny)]

    def second_sends():
        for slot, which in sent_early:
            copy_of(0, slot, which, sibling).wait_send()
        copy_of(0, slot_of(1, 0, 0), V, x_peer).start()
        for j in range(1, ny):
            copy_of(0, slot_of(0, ny - j, 0), K, y_peers[j]).start()

    def first_arrivals():
        beside = slot_of(1, 0, 0)
        arrive(beside, K)
        for j in range(1, ny):
            copy_of(beside, slot_of(1, ny - j, 0), K, y_peers[j]).start()
        to_sibling(beside, K)
        for yr in range(ny - 1, 0, -1):
            along = slot_of(0, yr, 0)
            arrive(along, V)
            copy_of(along, slot_of(1, yr, 0), V, x_peer).start()
            to_sibling(along, V)
        arrive(beside, V)
        to_sibling(beside, V)
        for yr in range(ny - 1, 0, -1):
            along = slot_of(0, yr, 0)
            arrive(along, K)
            to_sibling(along, K)

    to_exponent = math.log2(math.e) / math.sqrt(head)

    def step(t, carry):
        pl.when(t == 1)(second_sends)
        pl.when(t == 2)(first_arrivals)
        for yr in range(1, ny):
            @pl.when(t == slot_of(1, yr, 0))
            def _():
                for which in (K, V):
                    arrive(slot_of(1, yr, 0), which)
                    to_sibling(slot_of(1, yr, 0), which)

        @pl.when(t % 2 == 1)
        def _():
            arrive(t, K)
            arrive(t, V)

        scores = lax.dot_general(
            kv[t, K], q_vm[...], (((1,), (1,)), ((), ())), preferred_element_type=jnp.float32
        ) * to_exponent
        peak = jnp.maximum(peak_ref[...], jnp.max(scores, axis=0, keepdims=True))
        factor = jnp.exp2(peak_ref[...] - peak)
        probs = jnp.exp2(scores - peak)
        peak_ref[...] = peak
        total_ref[...] = total_ref[...] * factor + jnp.sum(probs, axis=0, keepdims=True)
        sum_ref[...] = sum_ref[...] * factor + lax.dot_general(
            kv[t, V], probs.astype(jnp.bfloat16), (((0,), (0,)), ((), ())), preferred_element_type=jnp.float32
        )
        return carry

    lax.fori_loop(0, 4 * ny, step, 0)

    is_peak = lax.broadcasted_iota(jnp.int32, (8, half), 0) < 4
    stat = jnp.where(is_peak, peak_ref[...], total_ref[...])
    for zt in range(nz):
        send_stat[zt] = stat[:, zt * rows:(zt + 1) * rows]
        send_acc[zt] = sum_ref[:, zt * rows:(zt + 1) * rows].T.astype(jnp.bfloat16)
    piece = rows // 2
    parts = []

    def part_copy(j, at):
        target = lax.rem(z + j, nz)
        src, dst = (send_stat, recv_stat) if at == 2 else (send_acc, recv_acc)
        src, dst = src.at[target], dst.at[nz - j]
        if at < 2:
            src, dst = src.at[pl.ds(at * piece, piece)], dst.at[pl.ds(at * piece, piece)]
        return pltpu.make_async_remote_copy(
            src_ref=src,
            dst_ref=dst,
            send_sem=z_send.at[j, at],
            recv_sem=z_recv.at[nz - j, at],
            device_id=z_peer(j),
            device_id_type=MESH,
        )

    for at in (2, 0, 1):
        for j in range(1, nz):
            copy = part_copy(j, at)
            copy.start()
            parts.append(copy)

    def block(xs, zs, at):
        return out_ref.at[pl.ds(pl.multiple_of((xs * nz + zs) * rows + at * piece, piece), piece)]

    shared = []

    def share(xr, zs, peer, way, at):
        xs = x if way == "z" and xr == 0 or way == "x" and xr == 1 else 1 - x
        return pltpu.make_async_remote_copy(
            src_ref=block(xs, zs, at),
            dst_ref=block(xs, zs, at),
            send_sem=g_send.at[min(len(shared), 4 * nz - 3)],
            recv_sem=g_recv.at[xr, zs, at],
            device_id=peer,
            device_id_type=MESH,
        )

    def begin(*args):
        copy = share(*args)
        copy.start()
        shared.append(copy)

    def landed(xr, zs, at):
        share(xr, zs, x_peer, "z", at).wait_recv()

    near = z + 1 - 2 * (z % 2)
    far = [(lax.rem(z // 2 + p, nz // 2) * 2 + b) for p in range(1, nz // 2) for b in range(2)]

    for j in range(1, nz):
        part_copy(j, 2).wait_recv()
    stats = [send_stat[z]] + [recv_stat[s] for s in range(1, nz)]
    joint_peak = functools.reduce(jnp.maximum, [s[0:1] for s in stats])
    factors = [jnp.exp2(s[0:1] - joint_peak) for s in stats]
    joint_total = sum(s[4:5] * f for s, f in zip(stats, factors))
    columns = [jnp.broadcast_to(f, (8, rows)).T[:, 0:1] for f in factors]
    total_column = jnp.broadcast_to(joint_total, (8, rows)).T[:, 0:1]

    for at in range(2):
        for j in range(1, nz):
            part_copy(j, at).wait_recv()
        span = slice(at * piece, (at + 1) * piece)
        sums = [send_acc[z, span]] + [recv_acc[s, span] for s in range(1, nz)]
        joint_sum = sum(a.astype(jnp.float32) * c[span] for a, c in zip(sums, columns))
        block(x, z, at)[...] = (joint_sum / total_column[span]).astype(jnp.bfloat16)
        begin(1, z, x_peer, "x", at)
        for zt in far + [near]:
            begin(0, z, (zt * 2 + x, inner), "z", at)
    for at in range(2):
        landed(1, z, at)
        begin(1, z, (near * 2 + x, inner), "z", at)
        for zs in far:
            landed(0, zs, at)
            begin(1, zs, x_peer, "x", at)
    for at in range(2):
        landed(0, near, at)
        for zs in [near] + far:
            landed(1, zs, at)
    for copy in parts + shared:
        copy.wait_send()
    for slot in range(1, 4 * ny):
        for which in (K, V):
            if (slot, which) in sent_early:
                continue
            copy_of(0, slot, which, sibling).wait_send()


def on_device(outer_size, inner_size, queries, key_rows, value_rows):
    count, head = queries.shape
    keys = key_rows.shape[0]
    nz, ny = outer_size // 2, inner_size // 2
    rows = count // 2 // nz
    dma = pltpu.SemaphoreType.DMA
    return pl.pallas_call(
        functools.partial(kernel, outer_size, inner_size),
        out_shape=jax.ShapeDtypeStruct((count, head), jnp.bfloat16),
        in_specs=[pl.BlockSpec(memory_space=pltpu.HBM)] * 3,
        out_specs=pl.BlockSpec(memory_space=pltpu.VMEM),
        scratch_shapes=[
            pltpu.VMEM((count // 2, head), jnp.bfloat16),
            pltpu.VMEM((4 * ny, 2, keys, head), jnp.bfloat16),
            pltpu.VMEM((head, count // 2), jnp.float32),
            pltpu.VMEM((1, count // 2), jnp.float32),
            pltpu.VMEM((1, count // 2), jnp.float32),
            pltpu.VMEM((nz, rows, head), jnp.bfloat16),
            pltpu.VMEM((nz, rows, head), jnp.bfloat16),
            pltpu.VMEM((nz, 8, rows), jnp.float32),
            pltpu.VMEM((nz, 8, rows), jnp.float32),
            dma((3,)),
            dma((4 * ny, 2)),
            dma((4 * ny, 2)),
            dma((nz, 3)),
            dma((nz, 3)),
            dma((4 * nz - 2,)),
            dma((2, nz, 2)),
        ],
        compiler_params=pltpu.CompilerParams(
            collective_id=0, has_side_effects=True, vmem_limit_bytes=48 * 1024 * 1024
        ),
        cost_estimate=pl.CostEstimate(
            flops=2 * count * keys * inner_size * head * 2,
            bytes_accessed=2 * (2 * count + 2 * keys) * head,
            transcendentals=count * keys * inner_size,
        ),
    )(*(pltpu.with_memory_space_constraint(a, pltpu.HBM) for a in (queries, key_rows, value_rows)))


def solution(mesh):
    return jax.shard_map(
        functools.partial(on_device, mesh.shape["outer"], mesh.shape["inner"]),
        mesh=mesh,
        in_specs=(P("inner", None), P(("outer", "inner"), None), P(("outer", "inner"), None)),
        out_specs=P("inner", None),
        check_vma=False,
    )
```

```python
import functools
import math

import jax
import jax.numpy as jnp
from jax import lax
from jax.experimental import pallas as pl
from jax.experimental.pallas import tpu as pltpu
from jax.sharding import PartitionSpec as P

MESH = pl.DeviceIdType.MESH
K, V = 0, 1


def kernel(outer_size, inner_size, q_hbm, k_hbm, v_hbm, out_ref, q_vm, q_turned, kv, sum_ref, peak_ref, total_ref,
           send_acc, recv_acc, send_stat, recv_stat, local_sem, kv_send, kv_recv, z_send, z_recv, g_send, g_recv):
    nz, ny = outer_size // 2, inner_size // 2
    queries, head = out_ref.shape
    half = queries // 2
    rows = half // nz
    outer, inner = lax.axis_index("outer"), lax.axis_index("inner")
    z, x = outer // 2, outer % 2
    y, core = inner // 2, inner % 2

    x_peer = (z * 2 + (1 - x), inner)
    sibling = (outer, y * 2 + (1 - core))
    y_peers = [None] + [(outer, lax.rem(y + j, ny) * 2 + core) for j in range(1, ny)]
    z_peers = [None] + [(lax.rem(z + j, nz) * 2 + x, inner) for j in range(1, nz)]

    def z_peer(j):
        return z_peers[j]

    def slot_of(xr, yr, c):
        chip = (xr if yr == 0 else 1 + yr) if xr == 0 or yr == 0 else ny + yr
        return chip * 2 + c

    local = [
        pltpu.make_async_copy(k_hbm, kv.at[0, K], local_sem.at[0]),
        pltpu.make_async_copy(v_hbm, kv.at[0, V], local_sem.at[1]),
        pltpu.make_async_copy(q_hbm.at[pl.ds(pl.multiple_of(x * half, half), half)], q_vm, local_sem.at[2]),
    ]
    for copy in local:
        copy.start()

    barrier = pltpu.get_barrier_semaphore()
    peers = [x_peer, sibling] + y_peers[1:] + z_peers[1:]
    for peer in peers:
        pl.semaphore_signal(barrier, inc=1, device_id=peer, device_id_type=MESH)
    peak_ref[...] = jnp.full_like(peak_ref, -1e30)
    total_ref[...] = jnp.zeros_like(total_ref)
    sum_ref[...] = jnp.zeros_like(sum_ref)
    local[0].wait()
    local[1].wait()
    pl.semaphore_wait(barrier, len(peers))

    def copy_of(source, slot, which, peer):
        return pltpu.make_async_remote_copy(
            src_ref=kv.at[source, which],
            dst_ref=kv.at[slot, which],
            send_sem=kv_send.at[slot, which],
            recv_sem=kv_recv.at[slot, which],
            device_id=peer,
            device_id_type=MESH,
        )

    def arrive(slot, which):
        copy_of(0, slot, which, sibling).wait_recv()

    def to_sibling(slot, which):
        copy_of(slot, slot + 1, which, sibling).start()

    copy_of(0, slot_of(1, 0, 0), K, x_peer).start()
    for j in range(1, ny):
        copy_of(0, slot_of(0, ny - j, 0), V, y_peers[j]).start()
    to_sibling(0, K)
    to_sibling(0, V)
    local[2].wait()
    q_turned[...] = q_vm[...].T
    tile = math.gcd(half, 128)
    sent_early = [(slot_of(1, 0, 0), K)] + [(slot_of(0, yr, 0), V) for yr in range(1, ny)]

    def second_sends():
        for slot, which in sent_early:
            copy_of(0, slot, which, sibling).wait_send()
        copy_of(0, slot_of(1, 0, 0), V, x_peer).start()
        for j in range(1, ny):
            copy_of(0, slot_of(0, ny - j, 0), K, y_peers[j]).start()

    def first_arrivals():
        beside = slot_of(1, 0, 0)
        arrive(beside, K)
        for j in range(1, ny):
            copy_of(beside, slot_of(1, ny - j, 0), K, y_peers[j]).start()
        to_sibling(beside, K)
        for yr in range(ny - 1, 0, -1):
            along = slot_of(0, yr, 0)
            arrive(along, V)
            copy_of(along, slot_of(1, yr, 0), V, x_peer).start()
            to_sibling(along, V)
        arrive(beside, V)
        to_sibling(beside, V)
        for yr in range(ny - 1, 0, -1):
            along = slot_of(0, yr, 0)
            arrive(along, K)
            to_sibling(along, K)

    to_exponent = math.log2(math.e) / math.sqrt(head)

    def step(t, carry):
        pl.when(t == 1)(second_sends)
        pl.when(t == 2)(first_arrivals)
        for yr in range(1, ny):
            @pl.when(t == slot_of(1, yr, 0))
            def _():
                for which in (K, V):
                    arrive(slot_of(1, yr, 0), which)
                    to_sibling(slot_of(1, yr, 0), which)

        @pl.when(t % 2 == 1)
        def _():
            arrive(t, K)
            arrive(t, V)

        keys, values = kv[t, K], kv[t, V].T
        for at in range(0, half, tile):
            span = slice(at, at + tile)
            scores = jnp.dot(keys, q_turned[:, span], preferred_element_type=jnp.float32) * to_exponent
            old_peak = peak_ref[:, span]
            peak = jnp.maximum(old_peak, jnp.max(scores, axis=0, keepdims=True))
            factor = jnp.exp2(old_peak - peak)
            probs = jnp.exp2(scores - peak)
            peak_ref[:, span] = peak
            total_ref[:, span] = total_ref[:, span] * factor + jnp.sum(probs, axis=0, keepdims=True)
            sum_ref[:, span] = sum_ref[:, span] * factor + jnp.dot(
                values, probs.astype(jnp.bfloat16), preferred_element_type=jnp.float32
            )
        return carry

    lax.fori_loop(0, 4 * ny, step, 0)

    is_peak = lax.broadcasted_iota(jnp.int32, (8, half), 0) < 4
    stat = jnp.where(is_peak, peak_ref[...], total_ref[...])
    for zt in range(nz):
        send_stat[zt] = stat[:, zt * rows:(zt + 1) * rows]
        send_acc[zt] = sum_ref[:, zt * rows:(zt + 1) * rows].T.astype(jnp.bfloat16)
    piece = rows // 2
    parts = []

    def part_copy(j, at):
        target = lax.rem(z + j, nz)
        src, dst = (send_stat, recv_stat) if at == 2 else (send_acc, recv_acc)
        src, dst = src.at[target], dst.at[nz - j]
        if at < 2:
            src, dst = src.at[pl.ds(at * piece, piece)], dst.at[pl.ds(at * piece, piece)]
        return pltpu.make_async_remote_copy(
            src_ref=src,
            dst_ref=dst,
            send_sem=z_send.at[j, at],
            recv_sem=z_recv.at[nz - j, at],
            device_id=z_peer(j),
            device_id_type=MESH,
        )

    for at in (2, 0, 1):
        for j in range(1, nz):
            copy = part_copy(j, at)
            copy.start()
            parts.append(copy)

    def block(xs, zs, at):
        return out_ref.at[pl.ds(pl.multiple_of((xs * nz + zs) * rows + at * piece, piece), piece)]

    shared = []

    def share(xr, zs, peer, way, at):
        xs = x if way == "z" and xr == 0 or way == "x" and xr == 1 else 1 - x
        return pltpu.make_async_remote_copy(
            src_ref=block(xs, zs, at),
            dst_ref=block(xs, zs, at),
            send_sem=g_send.at[min(len(shared), 4 * nz - 3)],
            recv_sem=g_recv.at[xr, zs, at],
            device_id=peer,
            device_id_type=MESH,
        )

    def begin(*args):
        copy = share(*args)
        copy.start()
        shared.append(copy)

    def landed(xr, zs, at):
        share(xr, zs, x_peer, "z", at).wait_recv()

    near = z + 1 - 2 * (z % 2)
    far = [(lax.rem(z // 2 + p, nz // 2) * 2 + b) for p in range(1, nz // 2) for b in range(2)]

    for j in range(1, nz):
        part_copy(j, 2).wait_recv()
    stats = [send_stat[z]] + [recv_stat[s] for s in range(1, nz)]
    joint_peak = functools.reduce(jnp.maximum, [s[0:1] for s in stats])
    factors = [jnp.exp2(s[0:1] - joint_peak) for s in stats]
    joint_total = sum(s[4:5] * f for s, f in zip(stats, factors))
    columns = [jnp.broadcast_to(f, (8, rows)).T[:, 0:1] for f in factors]
    total_column = jnp.broadcast_to(joint_total, (8, rows)).T[:, 0:1]

    for at in range(2):
        for j in range(1, nz):
            part_copy(j, at).wait_recv()
        span = slice(at * piece, (at + 1) * piece)
        sums = [send_acc[z, span]] + [recv_acc[s, span] for s in range(1, nz)]
        joint_sum = sum(a.astype(jnp.float32) * c[span] for a, c in zip(sums, columns))
        block(x, z, at)[...] = (joint_sum / total_column[span]).astype(jnp.bfloat16)
        begin(1, z, x_peer, "x", at)
        for zt in far + [near]:
            begin(0, z, (zt * 2 + x, inner), "z", at)
    for at in range(2):
        landed(1, z, at)
        begin(1, z, (near * 2 + x, inner), "z", at)
        for zs in far:
            landed(0, zs, at)
            begin(1, zs, x_peer, "x", at)
    for at in range(2):
        landed(0, near, at)
        for zs in [near] + far:
            landed(1, zs, at)
    for copy in parts + shared:
        copy.wait_send()
    for slot in range(1, 4 * ny):
        for which in (K, V):
            if (slot, which) in sent_early:
                continue
            copy_of(0, slot, which, sibling).wait_send()


def on_device(outer_size, inner_size, queries, key_rows, value_rows):
    count, head = queries.shape
    keys = key_rows.shape[0]
    nz, ny = outer_size // 2, inner_size // 2
    rows = count // 2 // nz
    dma = pltpu.SemaphoreType.DMA
    return pl.pallas_call(
        functools.partial(kernel, outer_size, inner_size),
        out_shape=jax.ShapeDtypeStruct((count, head), jnp.bfloat16),
        in_specs=[pl.BlockSpec(memory_space=pltpu.HBM)] * 3,
        out_specs=pl.BlockSpec(memory_space=pltpu.VMEM),
        scratch_shapes=[
            pltpu.VMEM((count // 2, head), jnp.bfloat16),
            pltpu.VMEM((head, count // 2), jnp.bfloat16),
            pltpu.VMEM((4 * ny, 2, keys, head), jnp.bfloat16),
            pltpu.VMEM((head, count // 2), jnp.float32),
            pltpu.VMEM((1, count // 2), jnp.float32),
            pltpu.VMEM((1, count // 2), jnp.float32),
            pltpu.VMEM((nz, rows, head), jnp.bfloat16),
            pltpu.VMEM((nz, rows, head), jnp.bfloat16),
            pltpu.VMEM((nz, 8, rows), jnp.float32),
            pltpu.VMEM((nz, 8, rows), jnp.float32),
            dma((3,)),
            dma((4 * ny, 2)),
            dma((4 * ny, 2)),
            dma((nz, 3)),
            dma((nz, 3)),
            dma((4 * nz - 2,)),
            dma((2, nz, 2)),
        ],
        compiler_params=pltpu.CompilerParams(
            collective_id=0, has_side_effects=True, vmem_limit_bytes=48 * 1024 * 1024
        ),
        cost_estimate=pl.CostEstimate(
            flops=2 * count * keys * inner_size * head * 2,
            bytes_accessed=2 * (2 * count + 2 * keys) * head,
            transcendentals=count * keys * inner_size,
        ),
    )(*(pltpu.with_memory_space_constraint(a, pltpu.HBM) for a in (queries, key_rows, value_rows)))


def solution(mesh):
    return jax.shard_map(
        functools.partial(on_device, mesh.shape["outer"], mesh.shape["inner"]),
        mesh=mesh,
        in_specs=(P("inner", None), P(("outer", "inner"), None), P(("outer", "inner"), None)),
        out_specs=P("inner", None),
        check_vma=False,
    )
```

```python
import functools
import math

import jax
import jax.numpy as jnp
from jax import lax
from jax.experimental import pallas as pl
from jax.experimental.pallas import tpu as pltpu
from jax.sharding import PartitionSpec as P

MESH = pl.DeviceIdType.MESH
K, V = 0, 1


def kernel(outer_size, inner_size, q_hbm, k_hbm, v_hbm, out_ref, q_vm, q_turned, kv, sum_ref, peak_ref, total_ref,
           send_acc, recv_acc, send_stat, recv_stat, local_sem, kv_send, kv_recv, z_send, z_recv, g_send, g_recv):
    nz, ny = outer_size // 2, inner_size // 2
    queries, head = out_ref.shape
    half = queries // 2
    rows = half // nz
    outer, inner = lax.axis_index("outer"), lax.axis_index("inner")
    z, x = outer // 2, outer % 2
    y, core = inner // 2, inner % 2

    x_peer = (z * 2 + (1 - x), inner)
    sibling = (outer, y * 2 + (1 - core))
    y_peers = [None] + [(outer, lax.rem(y + j, ny) * 2 + core) for j in range(1, ny)]
    z_peers = [None] + [(lax.rem(z + j, nz) * 2 + x, inner) for j in range(1, nz)]

    def z_peer(j):
        return z_peers[j]

    def slot_of(xr, yr, c):
        chip = (xr if yr == 0 else 1 + yr) if xr == 0 or yr == 0 else ny + yr
        return chip * 2 + c

    local = [
        pltpu.make_async_copy(k_hbm, kv.at[0, K], local_sem.at[0]),
        pltpu.make_async_copy(v_hbm, kv.at[0, V], local_sem.at[1]),
        pltpu.make_async_copy(q_hbm.at[pl.ds(pl.multiple_of(x * half, half), half)], q_vm, local_sem.at[2]),
    ]
    for copy in local:
        copy.start()

    barrier = pltpu.get_barrier_semaphore()
    corners = [None] + [(z * 2 + (1 - x), lax.rem(y + j, ny) * 2 + core) for j in range(1, ny)]
    peers = [x_peer, sibling] + y_peers[1:] + corners[1:] + z_peers[1:]
    for peer in peers:
        pl.semaphore_signal(barrier, inc=1, device_id=peer, device_id_type=MESH)
    peak_ref[...] = jnp.full_like(peak_ref, -1e30)
    total_ref[...] = jnp.zeros_like(total_ref)
    sum_ref[...] = jnp.zeros_like(sum_ref)
    local[0].wait()
    local[1].wait()
    pl.semaphore_wait(barrier, len(peers))

    def copy_of(source, slot, which, peer):
        return pltpu.make_async_remote_copy(
            src_ref=kv.at[source, which],
            dst_ref=kv.at[slot, which],
            send_sem=kv_send.at[slot, which],
            recv_sem=kv_recv.at[slot, which],
            device_id=peer,
            device_id_type=MESH,
        )

    def arrive(slot, which):
        copy_of(0, slot, which, sibling).wait_recv()

    def to_sibling(slot, which):
        copy_of(slot, slot + 1, which, sibling).start()

    copy_of(0, slot_of(1, 0, 0), K, x_peer).start()
    for j in range(1, ny):
        copy_of(0, slot_of(0, ny - j, 0), V, y_peers[j]).start()
    to_sibling(0, K)
    to_sibling(0, V)
    local[2].wait()
    q_turned[...] = q_vm[...].T
    tile = math.gcd(half, 128)
    copy_of(0, slot_of(1, 0, 0), V, x_peer).start()
    for j in range(1, ny):
        copy_of(0, slot_of(0, ny - j, 0), K, y_peers[j]).start()
    for j in range(1, ny):
        for which in (K, V):
            copy_of(0, slot_of(1, ny - j, 0), which, corners[j]).start()

    def first_arrivals():
        beside = slot_of(1, 0, 0)
        arrive(beside, K)
        to_sibling(beside, K)
        for yr in range(ny - 1, 0, -1):
            along = slot_of(0, yr, 0)
            arrive(along, V)
            to_sibling(along, V)
        arrive(beside, V)
        to_sibling(beside, V)
        for yr in range(ny - 1, 0, -1):
            along = slot_of(0, yr, 0)
            arrive(along, K)
            to_sibling(along, K)

    to_exponent = math.log2(math.e) / math.sqrt(head)

    def step(t, carry):
        pl.when(t == 2)(first_arrivals)
        for yr in range(1, ny):
            @pl.when(t == slot_of(1, yr, 0))
            def _():
                for which in (K, V):
                    arrive(slot_of(1, yr, 0), which)
                    to_sibling(slot_of(1, yr, 0), which)

        @pl.when(t % 2 == 1)
        def _():
            arrive(t, K)
            arrive(t, V)

        keys, values = kv[t, K], kv[t, V].T
        for at in range(0, half, tile):
            span = slice(at, at + tile)
            scores = jnp.dot(keys, q_turned[:, span], preferred_element_type=jnp.float32) * to_exponent
            old_peak = peak_ref[:, span]
            peak = jnp.maximum(old_peak, jnp.max(scores, axis=0, keepdims=True))
            factor = jnp.exp2(old_peak - peak)
            probs = jnp.exp2(scores - peak)
            peak_ref[:, span] = peak
            total_ref[:, span] = total_ref[:, span] * factor + jnp.sum(probs, axis=0, keepdims=True)
            sum_ref[:, span] = sum_ref[:, span] * factor + jnp.dot(
                values, probs.astype(jnp.bfloat16), preferred_element_type=jnp.float32
            )
        return carry

    lax.fori_loop(0, 4 * ny, step, 0)

    is_peak = lax.broadcasted_iota(jnp.int32, (8, half), 0) < 4
    stat = jnp.where(is_peak, peak_ref[...], total_ref[...])
    for zt in range(nz):
        send_stat[zt] = stat[:, zt * rows:(zt + 1) * rows]
        send_acc[zt] = sum_ref[:, zt * rows:(zt + 1) * rows].T.astype(jnp.bfloat16)
    piece = rows // 2
    parts = []

    def part_copy(j, at):
        target = lax.rem(z + j, nz)
        src, dst = (send_stat, recv_stat) if at == 2 else (send_acc, recv_acc)
        src, dst = src.at[target], dst.at[nz - j]
        if at < 2:
            src, dst = src.at[pl.ds(at * piece, piece)], dst.at[pl.ds(at * piece, piece)]
        return pltpu.make_async_remote_copy(
            src_ref=src,
            dst_ref=dst,
            send_sem=z_send.at[j, at],
            recv_sem=z_recv.at[nz - j, at],
            device_id=z_peer(j),
            device_id_type=MESH,
        )

    for at in (2, 0, 1):
        for j in range(1, nz):
            copy = part_copy(j, at)
            copy.start()
            parts.append(copy)

    def block(xs, zs, at):
        return out_ref.at[pl.ds(pl.multiple_of((xs * nz + zs) * rows + at * piece, piece), piece)]

    shared = []

    def share(xr, zs, peer, way, at):
        xs = x if way == "z" and xr == 0 or way == "x" and xr == 1 else 1 - x
        return pltpu.make_async_remote_copy(
            src_ref=block(xs, zs, at),
            dst_ref=block(xs, zs, at),
            send_sem=g_send.at[min(len(shared), 4 * nz - 3)],
            recv_sem=g_recv.at[xr, zs, at],
            device_id=peer,
            device_id_type=MESH,
        )

    def begin(*args):
        copy = share(*args)
        copy.start()
        shared.append(copy)

    def landed(xr, zs, at):
        share(xr, zs, x_peer, "z", at).wait_recv()

    near = z + 1 - 2 * (z % 2)
    far = [(lax.rem(z // 2 + p, nz // 2) * 2 + b) for p in range(1, nz // 2) for b in range(2)]

    for j in range(1, nz):
        part_copy(j, 2).wait_recv()
    stats = [send_stat[z]] + [recv_stat[s] for s in range(1, nz)]
    joint_peak = functools.reduce(jnp.maximum, [s[0:1] for s in stats])
    factors = [jnp.exp2(s[0:1] - joint_peak) for s in stats]
    joint_total = sum(s[4:5] * f for s, f in zip(stats, factors))
    columns = [jnp.broadcast_to(f, (8, rows)).T[:, 0:1] for f in factors]
    total_column = jnp.broadcast_to(joint_total, (8, rows)).T[:, 0:1]

    for at in range(2):
        for j in range(1, nz):
            part_copy(j, at).wait_recv()
        span = slice(at * piece, (at + 1) * piece)
        sums = [send_acc[z, span]] + [recv_acc[s, span] for s in range(1, nz)]
        joint_sum = sum(a.astype(jnp.float32) * c[span] for a, c in zip(sums, columns))
        block(x, z, at)[...] = (joint_sum / total_column[span]).astype(jnp.bfloat16)
        begin(1, z, x_peer, "x", at)
        for zt in far + [near]:
            begin(0, z, (zt * 2 + x, inner), "z", at)
    for at in range(2):
        landed(1, z, at)
        begin(1, z, (near * 2 + x, inner), "z", at)
        for zs in far:
            landed(0, zs, at)
            begin(1, zs, x_peer, "x", at)
    for at in range(2):
        landed(0, near, at)
        for zs in [near] + far:
            landed(1, zs, at)
    for copy in parts + shared:
        copy.wait_send()
    for slot in range(1, 4 * ny):
        for which in (K, V):
            copy_of(0, slot, which, sibling).wait_send()


def on_device(outer_size, inner_size, queries, key_rows, value_rows):
    count, head = queries.shape
    keys = key_rows.shape[0]
    nz, ny = outer_size // 2, inner_size // 2
    rows = count // 2 // nz
    dma = pltpu.SemaphoreType.DMA
    return pl.pallas_call(
        functools.partial(kernel, outer_size, inner_size),
        out_shape=jax.ShapeDtypeStruct((count, head), jnp.bfloat16),
        in_specs=[pl.BlockSpec(memory_space=pltpu.HBM)] * 3,
        out_specs=pl.BlockSpec(memory_space=pltpu.VMEM),
        scratch_shapes=[
            pltpu.VMEM((count // 2, head), jnp.bfloat16),
            pltpu.VMEM((head, count // 2), jnp.bfloat16),
            pltpu.VMEM((4 * ny, 2, keys, head), jnp.bfloat16),
            pltpu.VMEM((head, count // 2), jnp.float32),
            pltpu.VMEM((1, count // 2), jnp.float32),
            pltpu.VMEM((1, count // 2), jnp.float32),
            pltpu.VMEM((nz, rows, head), jnp.bfloat16),
            pltpu.VMEM((nz, rows, head), jnp.bfloat16),
            pltpu.VMEM((nz, 8, rows), jnp.float32),
            pltpu.VMEM((nz, 8, rows), jnp.float32),
            dma((3,)),
            dma((4 * ny, 2)),
            dma((4 * ny, 2)),
            dma((nz, 3)),
            dma((nz, 3)),
            dma((4 * nz - 2,)),
            dma((2, nz, 2)),
        ],
        compiler_params=pltpu.CompilerParams(
            collective_id=0, has_side_effects=True, vmem_limit_bytes=48 * 1024 * 1024
        ),
        cost_estimate=pl.CostEstimate(
            flops=2 * count * keys * inner_size * head * 2,
            bytes_accessed=2 * (2 * count + 2 * keys) * head,
            transcendentals=count * keys * inner_size,
        ),
    )(*(pltpu.with_memory_space_constraint(a, pltpu.HBM) for a in (queries, key_rows, value_rows)))


def solution(mesh):
    return jax.shard_map(
        functools.partial(on_device, mesh.shape["outer"], mesh.shape["inner"]),
        mesh=mesh,
        in_specs=(P("inner", None), P(("outer", "inner"), None), P(("outer", "inner"), None)),
        out_specs=P("inner", None),
        check_vma=False,
    )
```

```python
import functools
import math

import jax
import jax.numpy as jnp
from jax import lax
from jax.experimental import pallas as pl
from jax.experimental.pallas import tpu as pltpu
from jax.sharding import PartitionSpec as P

MESH = pl.DeviceIdType.MESH
K, V = 0, 1


def kernel(outer_size, inner_size, q_hbm, k_hbm, v_hbm, out_ref, q_vm, q_turned, kv, sum_ref, peak_ref, total_ref,
           send_acc, recv_acc, send_stat, recv_stat, local_sem, kv_send, kv_recv, z_send, z_recv, g_send, g_recv):
    nz, ny = outer_size // 2, inner_size // 2
    queries, head = out_ref.shape
    half = queries // 2
    rows = half // nz
    outer, inner = lax.axis_index("outer"), lax.axis_index("inner")
    z, x = outer // 2, outer % 2
    y, core = inner // 2, inner % 2

    x_peer = (z * 2 + (1 - x), inner)
    sibling = (outer, y * 2 + (1 - core))
    y_peers = [None] + [(outer, lax.rem(y + j, ny) * 2 + core) for j in range(1, ny)]
    z_peers = [None] + [(lax.rem(z + j, nz) * 2 + x, inner) for j in range(1, nz)]

    def z_peer(j):
        return z_peers[j]

    def slot_of(xr, yr, c):
        chip = (xr if yr == 0 else 1 + yr) if xr == 0 or yr == 0 else ny + yr
        return chip * 2 + c

    local = [
        pltpu.make_async_copy(k_hbm, kv.at[0, K], local_sem.at[0]),
        pltpu.make_async_copy(v_hbm, kv.at[0, V], local_sem.at[1]),
        pltpu.make_async_copy(q_hbm.at[pl.ds(pl.multiple_of(x * half, half), half)], q_vm, local_sem.at[2]),
    ]
    for copy in local:
        copy.start()

    barrier = pltpu.get_barrier_semaphore()
    corners = [None] + [(z * 2 + (1 - x), lax.rem(y + j, ny) * 2 + core) for j in range(1, ny)]
    peers = [x_peer, sibling] + y_peers[1:] + corners[1:] + z_peers[1:]
    peers += [(lax.rem(z + j, nz) * 2 + (1 - x), inner) for j in range(1, nz)]
    for peer in peers:
        pl.semaphore_signal(barrier, inc=1, device_id=peer, device_id_type=MESH)
    peak_ref[...] = jnp.full_like(peak_ref, -1e30)
    total_ref[...] = jnp.zeros_like(total_ref)
    sum_ref[...] = jnp.zeros_like(sum_ref)
    local[0].wait()
    local[1].wait()
    pl.semaphore_wait(barrier, len(peers))

    def copy_of(source, slot, which, peer):
        return pltpu.make_async_remote_copy(
            src_ref=kv.at[source, which],
            dst_ref=kv.at[slot, which],
            send_sem=kv_send.at[slot, which],
            recv_sem=kv_recv.at[slot, which],
            device_id=peer,
            device_id_type=MESH,
        )

    def arrive(slot, which):
        copy_of(0, slot, which, sibling).wait_recv()

    def to_sibling(slot, which):
        copy_of(slot, slot + 1, which, sibling).start()

    copy_of(0, slot_of(1, 0, 0), K, x_peer).start()
    for j in range(1, ny):
        copy_of(0, slot_of(0, ny - j, 0), V, y_peers[j]).start()
    to_sibling(0, K)
    to_sibling(0, V)
    local[2].wait()
    q_turned[...] = q_vm[...].T
    tile = math.gcd(half, 128)
    copy_of(0, slot_of(1, 0, 0), V, x_peer).start()
    for j in range(1, ny):
        copy_of(0, slot_of(0, ny - j, 0), K, y_peers[j]).start()
    for j in range(1, ny):
        for which in (K, V):
            copy_of(0, slot_of(1, ny - j, 0), which, corners[j]).start()

    def first_arrivals():
        beside = slot_of(1, 0, 0)
        arrive(beside, K)
        to_sibling(beside, K)
        for yr in range(ny - 1, 0, -1):
            along = slot_of(0, yr, 0)
            arrive(along, V)
            to_sibling(along, V)
        arrive(beside, V)
        to_sibling(beside, V)
        for yr in range(ny - 1, 0, -1):
            along = slot_of(0, yr, 0)
            arrive(along, K)
            to_sibling(along, K)

    to_exponent = math.log2(math.e) / math.sqrt(head)

    def step(t, carry):
        pl.when(t == 2)(first_arrivals)
        for yr in range(1, ny):
            @pl.when(t == slot_of(1, yr, 0))
            def _():
                for which in (K, V):
                    arrive(slot_of(1, yr, 0), which)
                    to_sibling(slot_of(1, yr, 0), which)

        @pl.when(t % 2 == 1)
        def _():
            arrive(t, K)
            arrive(t, V)

        keys, values = kv[t, K], kv[t, V].T
        for at in range(0, half, tile):
            span = slice(at, at + tile)
            scores = jnp.dot(keys, q_turned[:, span], preferred_element_type=jnp.float32) * to_exponent
            old_peak = peak_ref[:, span]
            peak = jnp.maximum(old_peak, jnp.max(scores, axis=0, keepdims=True))
            factor = jnp.exp2(old_peak - peak)
            probs = jnp.exp2(scores - peak)
            peak_ref[:, span] = peak
            total_ref[:, span] = total_ref[:, span] * factor + jnp.sum(probs, axis=0, keepdims=True)
            sum_ref[:, span] = sum_ref[:, span] * factor + jnp.dot(
                values, probs.astype(jnp.bfloat16), preferred_element_type=jnp.float32
            )
        return carry

    lax.fori_loop(0, 4 * ny, step, 0)

    is_peak = lax.broadcasted_iota(jnp.int32, (8, half), 0) < 4
    stat = jnp.where(is_peak, peak_ref[...], total_ref[...])
    for zt in range(nz):
        send_stat[zt] = stat[:, zt * rows:(zt + 1) * rows]
        send_acc[zt] = sum_ref[:, zt * rows:(zt + 1) * rows].T.astype(jnp.bfloat16)
    piece = rows // 2
    parts = []

    def part_copy(j, at):
        target = lax.rem(z + j, nz)
        src, dst = (send_stat, recv_stat) if at == 2 else (send_acc, recv_acc)
        src, dst = src.at[target], dst.at[nz - j]
        if at < 2:
            src, dst = src.at[pl.ds(at * piece, piece)], dst.at[pl.ds(at * piece, piece)]
        return pltpu.make_async_remote_copy(
            src_ref=src,
            dst_ref=dst,
            send_sem=z_send.at[j, at],
            recv_sem=z_recv.at[nz - j, at],
            device_id=z_peer(j),
            device_id_type=MESH,
        )

    for at in (2, 0, 1):
        for j in range(1, nz):
            copy = part_copy(j, at)
            copy.start()
            parts.append(copy)

    def block(xs, zs, at):
        return out_ref.at[pl.ds(pl.multiple_of((xs * nz + zs) * rows + at * piece, piece), piece)]

    shared = []

    def share(xr, zs, peer, way, at):
        xs = x if way == "z" and xr == 0 or way == "x" and xr == 1 else 1 - x
        return pltpu.make_async_remote_copy(
            src_ref=block(xs, zs, at),
            dst_ref=block(xs, zs, at),
            send_sem=g_send.at[min(len(shared), 4 * nz - 3)],
            recv_sem=g_recv.at[xr, zs, at],
            device_id=peer,
            device_id_type=MESH,
        )

    def begin(*args):
        copy = share(*args)
        copy.start()
        shared.append(copy)

    def landed(xr, zs, at):
        share(xr, zs, x_peer, "z", at).wait_recv()

    near = z + 1 - 2 * (z % 2)
    far = [(lax.rem(z // 2 + p, nz // 2) * 2 + b) for p in range(1, nz // 2) for b in range(2)]

    for j in range(1, nz):
        part_copy(j, 2).wait_recv()
    stats = [send_stat[z]] + [recv_stat[s] for s in range(1, nz)]
    joint_peak = functools.reduce(jnp.maximum, [s[0:1] for s in stats])
    factors = [jnp.exp2(s[0:1] - joint_peak) for s in stats]
    joint_total = sum(s[4:5] * f for s, f in zip(stats, factors))
    columns = [jnp.broadcast_to(f, (8, rows)).T[:, 0:1] for f in factors]
    total_column = jnp.broadcast_to(joint_total, (8, rows)).T[:, 0:1]

    for at in range(2):
        for j in range(1, nz):
            part_copy(j, at).wait_recv()
        span = slice(at * piece, (at + 1) * piece)
        sums = [send_acc[z, span]] + [recv_acc[s, span] for s in range(1, nz)]
        joint_sum = sum(a.astype(jnp.float32) * c[span] for a, c in zip(sums, columns))
        block(x, z, at)[...] = (joint_sum / total_column[span]).astype(jnp.bfloat16)
        begin(1, z, x_peer, "x", at)
        for zt in far + [near]:
            begin(0, z, (zt * 2 + x, inner), "z", at)
            begin(1, z, (zt * 2 + (1 - x), inner), "x", at)
    for at in range(2):
        landed(1, z, at)
        for zs in [near] + far:
            landed(0, zs, at)
            landed(1, zs, at)
    for copy in parts + shared:
        copy.wait_send()
    for slot in range(1, 4 * ny):
        for which in (K, V):
            copy_of(0, slot, which, sibling).wait_send()


def on_device(outer_size, inner_size, queries, key_rows, value_rows):
    count, head = queries.shape
    keys = key_rows.shape[0]
    nz, ny = outer_size // 2, inner_size // 2
    rows = count // 2 // nz
    dma = pltpu.SemaphoreType.DMA
    return pl.pallas_call(
        functools.partial(kernel, outer_size, inner_size),
        out_shape=jax.ShapeDtypeStruct((count, head), jnp.bfloat16),
        in_specs=[pl.BlockSpec(memory_space=pltpu.HBM)] * 3,
        out_specs=pl.BlockSpec(memory_space=pltpu.VMEM),
        scratch_shapes=[
            pltpu.VMEM((count // 2, head), jnp.bfloat16),
            pltpu.VMEM((head, count // 2), jnp.bfloat16),
            pltpu.VMEM((4 * ny, 2, keys, head), jnp.bfloat16),
            pltpu.VMEM((head, count // 2), jnp.float32),
            pltpu.VMEM((1, count // 2), jnp.float32),
            pltpu.VMEM((1, count // 2), jnp.float32),
            pltpu.VMEM((nz, rows, head), jnp.bfloat16),
            pltpu.VMEM((nz, rows, head), jnp.bfloat16),
            pltpu.VMEM((nz, 8, rows), jnp.float32),
            pltpu.VMEM((nz, 8, rows), jnp.float32),
            dma((3,)),
            dma((4 * ny, 2)),
            dma((4 * ny, 2)),
            dma((nz, 3)),
            dma((nz, 3)),
            dma((4 * nz - 2,)),
            dma((2, nz, 2)),
        ],
        compiler_params=pltpu.CompilerParams(
            collective_id=0, has_side_effects=True, vmem_limit_bytes=48 * 1024 * 1024
        ),
        cost_estimate=pl.CostEstimate(
            flops=2 * count * keys * inner_size * head * 2,
            bytes_accessed=2 * (2 * count + 2 * keys) * head,
            transcendentals=count * keys * inner_size,
        ),
    )(*(pltpu.with_memory_space_constraint(a, pltpu.HBM) for a in (queries, key_rows, value_rows)))


def solution(mesh):
    return jax.shard_map(
        functools.partial(on_device, mesh.shape["outer"], mesh.shape["inner"]),
        mesh=mesh,
        in_specs=(P("inner", None), P(("outer", "inner"), None), P(("outer", "inner"), None)),
        out_specs=P("inner", None),
        check_vma=False,
    )
```
